32 devices in a mesh: grp: 2 (over y), mp: 16 (over z, x, core).
Axes of the slice: x: 2, y: 2, z: 4, core: 2. Of those that a mesh axis runs over, the one named last changes fastest.
Arguments:
- query_grad: bfloat16 [64, 8192], P('grp'), parts along dimension 0, may hold values from -0.0625 to 0.0625
- query_input: bfloat16 [64, 8192], P('grp'), parts along dimension 0, may hold values from -6 to 6
- query_ids: int32 [64], P('grp'), parts along dimension 0, may hold values from 0 to 7, never falling along the last dimension, each value on 1 to 8 neighbouring positions
- train_grad: bfloat16 [256, 8192], P('grp'), parts along dimension 0, may hold values from -0.0625 to 0.0625
- train_input: bfloat16 [256, 8192], P('grp'), parts along dimension 0, may hold values from -3 to 3
- train_ids: int32 [256], P('grp'), parts along dimension 0, may hold values from 0 to 15, never falling along the last dimension, each value on 1 to 16 neighbouring positions
- output_basis: bfloat16 [8192, 8192], P(None, 'mp'), may hold values from -0.0625 to 0.0625
- input_basis: bfloat16 [8192, 8192], P(None, 'mp'), may hold values from -0.0625 to 0.0625
- eigenvalues: float32 [8192, 8192], P('mp'), may hold values from 0.05 to 5
Outputs:
- scores: float32 [16, 16], P('grp'), parts along dimension 0
The draws below stay inside these ranges and needn't reach their ends.
There are 2 independent parts, one for each index of `grp`. The reference program is written for one: setup_inputs(seed, part) draws one part's arguments, and reference() takes and returns one part's arrays. A program takes and returns all parts, laid end to end along the dimension named above; an argument that names none is the same for every part. Nothing has to cross between parts.
Inputs may be any that keep to these rules, and one draw needn't show every extreme that they name: `query_ids`: each query is a run of consecutive tokens, 1 to 8 long, one of exactly 8; ids never fall. `train_ids`: each training example is a run of consecutive tokens, 1 to 16 long, one of exactly 16; ids never fall.
All inputs are finite; a program needn't handle non-finite values.
Results may differ from the reference program's by a relative error of at most 0.0049.
Values may be sent and summed in bfloat16 or wider, within the bound.
A program may use at most 256 MiB of HBM per device.

```python
import math
import jax
import jax.numpy as jnp
import numpy as np
from jax import lax

D = 8192
QUERIES = 8
QMOST = 8
TRAIN = 16
TMOST = 16
QTOK = 32
TTOK = 128


def block_scale(stream_key, dims, cuts, low, largest):
    gain, own = 1.0, jax.random.fold_in(stream_key, 6)
    for axis_at, parts in cuts:
        steps = jnp.exp(jax.random.uniform(jax.random.fold_in(own, axis_at), (parts,), jnp.float32, low / len(cuts), largest / len(cuts)))
        gain = gain * jnp.repeat(steps, dims[axis_at] // parts).reshape([-1 if axis == axis_at else 1 for axis in range(len(dims))])
    return gain


def profile(count, total, most, slope):
    weights = [(1 << 20) // math.isqrt(rank ** slope) + 1 for rank in range(2, count + 1)]
    surplus, given = total - most - (count - 1), [1] * (count - 1)
    while surplus > 0:
        movable = [i for i in range(count - 1) if given[i] < most]
        whole, budget = sum([weights[i] for i in movable]), surplus
        for i in movable:
            extra = min(most - given[i], max(1, budget * weights[i] // whole), surplus)
            given[i] = given[i] + extra
            surplus = surplus - extra
    return np.array([most] + given)


def uneven_parts(key, amount, total, reach, skew):
    if amount == 2:
        one = jax.random.randint(key, (), max(1, total - reach), min(reach, total - 1) + 1)
        return jnp.stack([one, total - one])
    tallies = jnp.asarray(profile(amount, total, reach, skew), jnp.int32)
    couples = (amount - 1) // 2
    donor, taker = tallies[1:1 + 2 * couples:2], tallies[2:2 + 2 * couples:2]
    slack = jnp.minimum(donor - 1, reach - taker)
    moved = jax.random.randint(jax.random.fold_in(key, 1), (couples,), 0, 1 << 20) % (slack + 1)
    tallies = tallies.at[1:1 + 2 * couples:2].set(donor - moved).at[2:2 + 2 * couples:2].set(taker + moved)
    return tallies[jax.random.permutation(jax.random.fold_in(key, 2), amount)]


def scatter_about(own_key, extent, deviation, most, cuts=(), kind=jnp.bfloat16):
    drawn = jax.random.normal(own_key, extent, jnp.float32) * deviation
    if len(cuts) > 0:
        drawn = block_scale(own_key, extent, cuts, -0.22, 0.18) * drawn
    return jnp.clip(drawn, min=-most, max=most).astype(kind)


def setup_inputs(seed: int = 0, part: int = 0) -> dict:
    key_of = jax.random.split(jax.random.key(seed), 10)
    part_splits = jax.random.split(jax.random.fold_in(key_of[9], part), 10)
    query_grad = scatter_about(part_splits[0], (QTOK, D), D ** -0.5, 0.0625)
    query_input = scatter_about(part_splits[1], (QTOK, D), 1.0, 6.0)
    query_ids = jnp.searchsorted(jnp.cumsum(uneven_parts(part_splits[2], QUERIES, QTOK, QMOST, 1)), jnp.arange(QTOK), side="right").astype(jnp.int32)
    train_grad = scatter_about(part_splits[3], (TTOK, D), D ** -0.5, 0.0625)
    train_input = scatter_about(part_splits[4], (TTOK, D), 0.5, 3.0)
    train_ids = jnp.searchsorted(jnp.cumsum(uneven_parts(part_splits[5], TRAIN, TTOK, TMOST, 1)), jnp.arange(TTOK), side="right").astype(jnp.int32)
    output_basis = scatter_about(key_of[6], (D, D), D ** -0.5, 0.0625, ((1, 16),))
    input_basis = scatter_about(key_of[7], (D, D), D ** -0.5, 0.0625, ((1, 16),))
    eigenvalues = jnp.clip(jnp.exp(math.log(5.0) - 4.6051702 * jax.random.uniform(key_of[8], (D, D), jnp.float32) ** block_scale(key_of[8], (D, D), ((0, 16),), -0.2, 0.2)), 0.05, 5.0)
    return dict(query_grad=query_grad, query_input=query_input, query_ids=query_ids, train_grad=train_grad, train_input=train_input, train_ids=train_ids, output_basis=output_basis, input_basis=input_basis, eigenvalues=eigenvalues)


damping_shift = 0.25


def rotate(factors, basis_wide):
    return jnp.dot(factors.astype(jnp.float32), basis_wide, precision=lax.Precision.HIGHEST).astype(jnp.bfloat16)


def reference(query_grad, query_input, query_ids, train_grad, train_input, train_ids, output_basis, input_basis, eigenvalues):
    output_wide = output_basis.astype(jnp.float32)
    input_wide = input_basis.astype(jnp.float32)
    query_left = rotate(query_grad, output_wide)
    query_right = rotate(query_input, input_wide)
    train_left = rotate(train_grad, output_wide)
    train_right = rotate(train_input, input_wide)
    labels = jnp.arange(QUERIES, dtype=jnp.int32)
    starts = jnp.sum((query_ids[None, :] < labels[:, None]).astype(jnp.int32), axis=1)
    window = jnp.minimum(starts[:, None] + jnp.arange(QMOST, dtype=jnp.int32)[None, :], query_ids.shape[0] - 1).astype(jnp.int32)
    live_slot = query_ids[window] == labels[:, None]
    train_onehot = (train_ids[:, None] == jnp.arange(TRAIN, dtype=jnp.int32)[None, :]).astype(jnp.float32)
    left_train = train_left.astype(jnp.float32)
    right_train = train_right.astype(jnp.float32)

    def score_query(query_label):
        slots = window[query_label]
        slot_live = live_slot[query_label]
        left_rows = jnp.where(slot_live[:, None], query_left[slots].astype(jnp.float32), jnp.zeros((), jnp.float32))
        right_rows = query_right[slots].astype(jnp.float32)
        products = jnp.dot(left_rows.T, right_rows, precision=lax.Precision.HIGHEST)
        precond = (products / (eigenvalues + damping_shift)).astype(jnp.bfloat16)
        precond = lax.optimization_barrier(precond).astype(jnp.float32)
        inner_rows = jnp.dot(left_train, precond, precision=lax.Precision.HIGHEST)
        contrib = jnp.sum(inner_rows * right_train, axis=1)
        return jnp.dot(contrib, train_onehot, precision=lax.Precision.HIGHEST)

    return lax.map(score_query, labels)
```

```python
import functools
import math

import jax
import jax.numpy as jnp
from jax import lax
from jax.experimental import pallas as pl
from jax.experimental.pallas import tpu as pltpu
from jax.sharding import PartitionSpec as P

QUERIES = 8
QMOST = 8
TRAIN = 16


damping_shift = 0.25


def rotate(basis, factors):
    return lax.dot_general(
        basis, factors, (((0,), (1,)), ((), ())), preferred_element_type=jnp.float32
    ).astype(jnp.bfloat16)


def query_window(query_ids):
    token_count = query_ids.shape[0]
    labels = jnp.arange(QUERIES, dtype=jnp.int32)
    starts = jnp.sum((query_ids[None, :] < labels[:, None]).astype(jnp.int32), axis=1)
    window = jnp.minimum(
        starts[:, None] + jnp.arange(QMOST, dtype=jnp.int32)[None, :], token_count - 1
    )
    live_slot = jnp.take(query_ids, window) == labels[:, None]
    return (window, live_slot)


def window_rows(columns, window):
    return jnp.transpose(jnp.take(columns, window, axis=1), (1, 2, 0))


def build_precond(left_window, right_cols, eig_cols, window):
    right_window = window_rows(right_cols, window)
    query_count = left_window.shape[0]
    group_size = math.gcd(query_count, 8)
    left_groups = left_window.reshape(
        (query_count // group_size, group_size) + left_window.shape[1:]
    )
    right_groups = right_window.reshape(
        (query_count // group_size, group_size) + right_window.shape[1:]
    )

    def one_group(operands):
        products = jnp.einsum(
            "qms,qma->qsa", operands[0], operands[1], preferred_element_type=jnp.float32
        )
        return (products / (eig_cols[None] + damping_shift)).astype(jnp.bfloat16)

    precond_groups = lax.map(one_group, (left_groups, right_groups))
    return precond_groups.reshape((query_count,) + precond_groups.shape[2:])


def on_device(
    query_grad,
    query_input,
    query_ids,
    train_grad,
    train_input,
    train_ids,
    output_basis,
    input_basis,
    eigenvalues,
):
    query_left = rotate(output_basis, query_grad)
    query_right = rotate(input_basis, query_input)
    train_left = rotate(output_basis, train_grad)
    train_right = rotate(input_basis, train_input)
    window, live_slot = query_window(query_ids)
    left_taken = window_rows(query_left, window)
    left_window = jnp.where(live_slot[:, :, None], left_taken, jnp.zeros((), jnp.bfloat16))
    right_full, train_full = (
        lax.all_gather(query_right, "mp", axis=0, tiled=True),
        lax.all_gather(train_right, "mp", axis=0, tiled=True),
    )
    precond = build_precond(left_window, right_full, eigenvalues, window)
    inner_sum = jnp.einsum("qsa,at->qst", precond, train_full, preferred_element_type=jnp.float32)
    contrib = jnp.einsum(
        "qst,st->qt", inner_sum, train_left.astype(jnp.float32), precision=lax.Precision.HIGHEST
    )
    onehot = (train_ids[:, None] == jnp.arange(TRAIN, dtype=jnp.int32)[None, :]).astype(jnp.float32)
    shares = jnp.dot(contrib, onehot, precision=lax.Precision.HIGHEST)
    return lax.psum(shares, "mp")


Z, X, C = 4, 2, 2
MP = Z * X * C
CHUNKS = 8
HALF = 256


def scores_kernel(
    qids_ref,
    tids_ref,
    qgrad,
    qin,
    tgrad,
    tin,
    obasis,
    ibasis,
    eig,
    out_ref,
    in_rows,
    grad_rows,
    ib,
    ob,
    ev,
    inv,
    total,
    rights,
    qleft,
    tleft,
    acc,
    shares,
    row_sem,
    ib_sem,
    ob_sem,
    ev_sem,
    send_sem,
    recv_sem,
    share_send,
    share_recv,
):
    me = lax.axis_index("mp")
    z, x, c = me // (X * C), (me // C) % X, me % C
    qtok, depth = qin.shape
    ttok = tin.shape[0]
    width = ibasis.shape[1]
    chunk = depth // CHUNKS

    def z_peer(d):
        return (z // 2 + d // 2) % 2 * 2 + (z % 2 + d % 2) % 2

    def index_of(d, dx, dc):
        return (z_peer(d) * X + (x + dx) % X) * C + (c + dc) % C

    def row_copies(q, t, rows, k):
        return (
            pltpu.make_async_copy(q, rows.at[pl.ds(0, qtok)], row_sem.at[k]),
            pltpu.make_async_copy(t, rows.at[pl.ds(qtok, ttok)], row_sem.at[k + 1]),
        )

    def basis_copy(source, target, sem, k):
        part = pl.ds(pl.multiple_of(k * chunk, chunk), chunk)
        return pltpu.make_async_copy(source.at[part], target.at[part], sem.at[k])

    def block_index(i):
        return index_of(i // 4, i % 4 // 2, i % 2)

    def eig_copy(i):
        j = block_index(i)
        part = pl.ds(pl.multiple_of(j * width, width), width)
        return pltpu.make_async_copy(eig.at[:, part], ev.at[j], ev_sem.at[j])

    for copy in row_copies(qin, tin, in_rows, 0):
        copy.start()
    for k in range(CHUNKS):
        basis_copy(ibasis, ib, ib_sem, k).start()
    for copy in row_copies(qgrad, tgrad, grad_rows, 2):
        copy.start()

    barrier = pltpu.get_barrier_semaphore()

    @pl.loop(1, MP)
    def _(k):
        pl.semaphore_signal(barrier, inc=1, device_id={"mp": (me + k) % MP})

    def rotate_rows(rows, basis, wait_chunk):
        total[...] = jnp.zeros_like(total)

        @pl.loop(0, CHUNKS)
        def _(k):
            wait_chunk(k)
            part = pl.ds(pl.multiple_of(k * chunk, chunk), chunk)
            total[...] += jnp.dot(rows[:, part], basis[part, :], preferred_element_type=jnp.float32)

    def wait_in(k):
        basis_copy(ibasis, ib, ib_sem, k).wait()
        basis_copy(obasis, ob, ob_sem, k).start()

    def wait_out(k):
        basis_copy(obasis, ob, ob_sem, k).wait()
        eig_copy(2 * k).start()
        eig_copy(2 * k + 1).start()

    for copy in row_copies(qin, tin, in_rows, 0):
        copy.wait()
    rotate_rows(in_rows, ib, wait_in)
    rights[me] = total[...].astype(jnp.bfloat16)

    pl.semaphore_wait(barrier, MP - 1)

    def send(j, peer, kind, d):
        return pltpu.make_async_remote_copy(
            src_ref=rights.at[j],
            dst_ref=rights.at[j],
            send_sem=send_sem.at[kind, d],
            recv_sem=recv_sem.at[j],
            device_id={"mp": peer},
        )

    x_peer, core_peer = index_of(0, 1, 0), index_of(0, 0, 1)
    send(me, core_peer, 2, 0).start()
    send(me, x_peer, 1, 0).start()
    for d in range(1, Z):
        send(me, index_of(d, 0, 0), 0, d).start()

    for copy in row_copies(qgrad, tgrad, grad_rows, 2):
        copy.wait()
    rotate_rows(grad_rows, ob, wait_out)
    tleft[...] = total[pl.ds(qtok, ttok), :].astype(jnp.bfloat16)
    turned = total[pl.ds(0, 128), :].astype(jnp.bfloat16).astype(jnp.float32).T[:, :qtok]
    qids = qids_ref[...]
    last = lax.broadcasted_iota(jnp.int32, (1, qtok), 1) == qtok - 1
    for q in range(QUERIES):
        start = jnp.sum(jnp.where(qids < q, 1.0, 0.0), axis=1, keepdims=True)
        repeats = jnp.where(last, start + (QMOST - qtok + 1), 1.0)
        weights = jnp.where(qids == q, repeats, 0.0)
        qleft[q] = (turned * weights).astype(jnp.bfloat16)
    acc[...] = jnp.zeros_like(acc)

    def arrived(j):
        send(j, core_peer, 0, 0).wait_recv()

    @pl.loop(0, MP)
    def _(i):
        d, r = i // 4, i % 4
        j = block_index(i)

        @pl.when(jnp.logical_and(r == 2, d < Z - 1))
        def _():
            nearer = index_of(d + 1, 0, 0)
            arrived(nearer)
            send(nearer, x_peer, 1, d + 1).start()
            send(nearer, core_peer, 2, d + 1).start()

        @pl.when(r == 1)
        def _():
            arrived(j)
            across = index_of(d, 1, 0)
            arrived(across)
            send(across, core_peer, 3, d).start()

        @pl.when(r == 3)
        def _():
            arrived(j)

        eig_copy(i).wait()
        inv[...] = 1.0 / (ev[j] + damping_shift)

        @pl.loop(0, QUERIES, unroll=UNROLL)
        def _(q):
            for h in range(0, width, HALF):
                part = pl.ds(h, HALF)
                products = jnp.dot(
                    qleft[q], rights[j, pl.ds(0, qtok), part], preferred_element_type=jnp.float32
                )
                precond = (products * inv[:, part]).astype(jnp.bfloat16)
                inner = jnp.dot(tleft[...], precond, preferred_element_type=jnp.float32)
                inner = inner * rights[j, pl.ds(qtok, ttok), part].astype(jnp.float32)
                folded = inner[:, :128]
                for lane in range(128, HALF, 128):
                    folded = folded + inner[:, lane : lane + 128]
                acc[q] += folded

    lanes = lax.broadcasted_iota(jnp.int32, (ttok, 128), 1)
    contrib = jnp.zeros((ttok, 128), jnp.float32)
    for q in range(QUERIES):
        contrib = jnp.where(lanes == q, jnp.sum(acc[q], axis=1, keepdims=True), contrib)
    labels = lax.broadcasted_iota(jnp.int32, (128, ttok), 0)
    onehot = jnp.where(labels == tids_ref[...], 1.0, 0.0)
    shares[me] = lax.dot_general(
        contrib.T[:QUERIES],
        onehot,
        (((1,), (1,)), ((), ())),
        precision=lax.Precision.HIGHEST,
        preferred_element_type=jnp.float32,
    )

    def share_copy(k, j):
        return pltpu.make_async_remote_copy(
            src_ref=shares.at[j],
            dst_ref=shares.at[j],
            send_sem=share_send.at[k],
            recv_sem=share_recv.at[j],
            device_id={"mp": (me + k) % MP},
        )

    @pl.loop(1, MP)
    def _(k):
        share_copy(k, me).start()

    for d in range(Z):
        if d > 0:
            send(me, index_of(d, 0, 0), 0, d).wait_send()
        send(me, x_peer, 1, d).wait_send()
        send(me, core_peer, 2, d).wait_send()
        send(me, core_peer, 3, d).wait_send()

    @pl.loop(1, MP)
    def _(k):
        share_copy(k, (me + k) % MP).wait_recv()

    @pl.loop(1, MP)
    def _(k):
        share_copy(k, me).wait_send()

    result = shares[0]
    for j in range(1, MP):
        result = result + shares[j]
    out_ref[...] = result[:, :TRAIN]


UNROLL = 4


def fused_scores(qgrad, qin, qids, tgrad, tin, tids, obasis, ibasis, eig):
    qtok, depth = qin.shape
    ttok = tin.shape[0]
    width = ibasis.shape[1]
    tokens = qtok + ttok
    vmem = pl.BlockSpec(memory_space=pltpu.VMEM)
    hbm = pl.BlockSpec(memory_space=pl.ANY)
    dma = pltpu.SemaphoreType.DMA
    return pl.pallas_call(
        scores_kernel,
        out_shape=jax.ShapeDtypeStruct((QUERIES, TRAIN), jnp.float32),
        in_specs=[vmem, vmem] + [hbm] * 7,
        out_specs=vmem,
        scratch_shapes=[
            pltpu.VMEM((tokens, depth), jnp.bfloat16),
            pltpu.VMEM((tokens, depth), jnp.bfloat16),
            pltpu.VMEM((depth, width), jnp.bfloat16),
            pltpu.VMEM((depth, width), jnp.bfloat16),
            pltpu.VMEM((MP, width, width), jnp.float32),
            pltpu.VMEM((width, width), jnp.float32),
            pltpu.VMEM((tokens, width), jnp.float32),
            pltpu.VMEM((MP, tokens, width), jnp.bfloat16),
            pltpu.VMEM((QUERIES, width, qtok), jnp.bfloat16),
            pltpu.VMEM((ttok, width), jnp.bfloat16),
            pltpu.VMEM((QUERIES, ttok, 128), jnp.float32),
            pltpu.VMEM((MP, QUERIES, 128), jnp.float32),
            dma((4,)),
            dma((CHUNKS,)),
            dma((CHUNKS,)),
            dma((MP,)),
            dma((4, Z)),
            dma((MP,)),
            dma((MP,)),
            dma((MP,)),
        ],
        compiler_params=pltpu.CompilerParams(
            collective_id=0, has_side_effects=True, vmem_limit_bytes=56 * 2**20
        ),
    )(qids.reshape(1, qtok), tids.reshape(1, ttok), qgrad, qin, tgrad, tin, obasis, ibasis, eig)


def device_part(mp, qgrad, qin, qids, tgrad, tin, tids, obasis, ibasis, eig):
    run = fused_scores if mp == MP else on_device
    return run(qgrad, qin, qids, tgrad, tin, tids, obasis, ibasis, eig)


def solution(mesh):
    return jax.shard_map(
        functools.partial(device_part, mesh.shape["mp"]),
        mesh=mesh,
        in_specs=(
            P("grp", None),
            P("grp", None),
            P("grp"),
            P("grp", None),
            P("grp", None),
            P("grp"),
            P(None, "mp"),
            P(None, "mp"),
            P("mp", None),
        ),
        out_specs=P("grp", None),
        check_vma=False,
    )
```

```python
import functools
import math

import jax
import jax.numpy as jnp
from jax import lax
from jax.experimental import pallas as pl
from jax.experimental.pallas import tpu as pltpu
from jax.sharding import PartitionSpec as P

QUERIES = 8
QMOST = 8
TRAIN = 16


damping_shift = 0.25


def rotate(basis, factors):
    return lax.dot_general(
        basis, factors, (((0,), (1,)), ((), ())), preferred_element_type=jnp.float32
    ).astype(jnp.bfloat16)


def query_window(query_ids):
    token_count = query_ids.shape[0]
    labels = jnp.arange(QUERIES, dtype=jnp.int32)
    starts = jnp.sum((query_ids[None, :] < labels[:, None]).astype(jnp.int32), axis=1)
    window = jnp.minimum(
        starts[:, None] + jnp.arange(QMOST, dtype=jnp.int32)[None, :], token_count - 1
    )
    live_slot = jnp.take(query_ids, window) == labels[:, None]
    return (window, live_slot)


def window_rows(columns, window):
    return jnp.transpose(jnp.take(columns, window, axis=1), (1, 2, 0))


def build_precond(left_window, right_cols, eig_cols, window):
    right_window = window_rows(right_cols, window)
    query_count = left_window.shape[0]
    group_size = math.gcd(query_count, 8)
    left_groups = left_window.reshape(
        (query_count // group_size, group_size) + left_window.shape[1:]
    )
    right_groups = right_window.reshape(
        (query_count // group_size, group_size) + right_window.shape[1:]
    )

    def one_group(operands):
        products = jnp.einsum(
            "qms,qma->qsa", operands[0], operands[1], preferred_element_type=jnp.float32
        )
        return (products / (eig_cols[None] + damping_shift)).astype(jnp.bfloat16)

    precond_groups = lax.map(one_group, (left_groups, right_groups))
    return precond_groups.reshape((query_count,) + precond_groups.shape[2:])


def on_device(
    query_grad,
    query_input,
    query_ids,
    train_grad,
    train_input,
    train_ids,
    output_basis,
    input_basis,
    eigenvalues,
):
    query_left = rotate(output_basis, query_grad)
    query_right = rotate(input_basis, query_input)
    train_left = rotate(output_basis, train_grad)
    train_right = rotate(input_basis, train_input)
    window, live_slot = query_window(query_ids)
    left_taken = window_rows(query_left, window)
    left_window = jnp.where(live_slot[:, :, None], left_taken, jnp.zeros((), jnp.bfloat16))
    right_full, train_full = (
        lax.all_gather(query_right, "mp", axis=0, tiled=True),
        lax.all_gather(train_right, "mp", axis=0, tiled=True),
    )
    precond = build_precond(left_window, right_full, eigenvalues, window)
    inner_sum = jnp.einsum("qsa,at->qst", precond, train_full, preferred_element_type=jnp.float32)
    contrib = jnp.einsum(
        "qst,st->qt", inner_sum, train_left.astype(jnp.float32), precision=lax.Precision.HIGHEST
    )
    onehot = (train_ids[:, None] == jnp.arange(TRAIN, dtype=jnp.int32)[None, :]).astype(jnp.float32)
    shares = jnp.dot(contrib, onehot, precision=lax.Precision.HIGHEST)
    return lax.psum(shares, "mp")


Z, X, C = 4, 2, 2
MP = Z * X * C
CHUNKS = 8


def scores_kernel(
    qids_ref,
    tids_ref,
    qgrad,
    qin,
    tgrad,
    tin,
    obasis,
    ibasis,
    eig,
    out_ref,
    in_rows,
    grad_rows,
    ib,
    ob,
    ev,
    inv,
    precond,
    total,
    rights,
    qleft,
    tleft,
    acc,
    shares,
    row_sem,
    ib_sem,
    ob_sem,
    ev_sem,
    send_sem,
    recv_sem,
    share_send,
    share_recv,
):
    me = lax.axis_index("mp")
    z, x, c = me // (X * C), (me // C) % X, me % C
    qtok, depth = qin.shape
    ttok = tin.shape[0]
    width = ibasis.shape[1]
    chunk = depth // CHUNKS

    def z_peer(d):
        return (z // 2 + d // 2) % 2 * 2 + (z % 2 + d % 2) % 2

    def index_of(d, dx, dc):
        return (z_peer(d) * X + (x + dx) % X) * C + (c + dc) % C

    def row_copies(q, t, rows, k):
        return (
            pltpu.make_async_copy(q, rows.at[pl.ds(0, qtok)], row_sem.at[k]),
            pltpu.make_async_copy(t, rows.at[pl.ds(qtok, ttok)], row_sem.at[k + 1]),
        )

    def basis_copy(source, target, sem, k):
        part = pl.ds(pl.multiple_of(k * chunk, chunk), chunk)
        return pltpu.make_async_copy(source.at[part], target.at[part], sem.at[k])

    def block_index(i):
        return index_of(i // 4, i % 4 // 2, i % 2)

    def eig_copy(i):
        j = block_index(i)
        part = pl.ds(pl.multiple_of(j * width, width), width)
        return pltpu.make_async_copy(eig.at[:, part], ev.at[j], ev_sem.at[j])

    for copy in row_copies(qin, tin, in_rows, 0):
        copy.start()
    for k in range(CHUNKS):
        basis_copy(ibasis, ib, ib_sem, k).start()
    for copy in row_copies(qgrad, tgrad, grad_rows, 2):
        copy.start()

    barrier = pltpu.get_barrier_semaphore()

    @pl.loop(1, MP)
    def _(k):
        pl.semaphore_signal(barrier, inc=1, device_id={"mp": (me + k) % MP})

    def rotate_rows(rows, basis, wait_chunk):
        total[...] = jnp.zeros_like(total)

        @pl.loop(0, CHUNKS)
        def _(k):
            wait_chunk(k)
            part = pl.ds(pl.multiple_of(k * chunk, chunk), chunk)
            total[...] += jnp.dot(rows[:, part], basis[part, :], preferred_element_type=jnp.float32)

    def wait_in(k):
        basis_copy(ibasis, ib, ib_sem, k).wait()
        basis_copy(obasis, ob, ob_sem, k).start()

    def wait_out(k):
        basis_copy(obasis, ob, ob_sem, k).wait()
        eig_copy(2 * k).start()
        eig_copy(2 * k + 1).start()

    for copy in row_copies(qin, tin, in_rows, 0):
        copy.wait()
    rotate_rows(in_rows, ib, wait_in)
    rights[me] = total[...].astype(jnp.bfloat16)

    pl.semaphore_wait(barrier, MP - 1)

    def send(j, peer, kind, d):
        return pltpu.make_async_remote_copy(
            src_ref=rights.at[j],
            dst_ref=rights.at[j],
            send_sem=send_sem.at[kind, d],
            recv_sem=recv_sem.at[j],
            device_id={"mp": peer},
        )

    x_peer, core_peer = index_of(0, 1, 0), index_of(0, 0, 1)
    send(me, core_peer, 2, 0).start()
    send(me, x_peer, 1, 0).start()
    for d in range(1, Z):
        send(me, index_of(d, 0, 0), 0, d).start()

    for copy in row_copies(qgrad, tgrad, grad_rows, 2):
        copy.wait()
    rotate_rows(grad_rows, ob, wait_out)
    tleft[...] = total[pl.ds(qtok, ttok), :].astype(jnp.bfloat16)
    turned = total[pl.ds(0, 128), :].astype(jnp.bfloat16).astype(jnp.float32).T[:, :qtok]
    qids = qids_ref[...]
    last = lax.broadcasted_iota(jnp.int32, (1, qtok), 1) == qtok - 1
    for q in range(QUERIES):
        start = jnp.sum(jnp.where(qids < q, 1.0, 0.0), axis=1, keepdims=True)
        repeats = jnp.where(last, start + (QMOST - qtok + 1), 1.0)
        weights = jnp.where(qids == q, repeats, 0.0)
        qleft[q] = (turned * weights).astype(jnp.bfloat16)
    acc[...] = jnp.zeros_like(acc)

    def arrived(j):
        send(j, core_peer, 0, 0).wait_recv()

    @pl.loop(0, MP)
    def _(i):
        d, r = i // 4, i % 4
        j = block_index(i)

        @pl.when(jnp.logical_and(r == 2, d < Z - 1))
        def _():
            nearer = index_of(d + 1, 0, 0)
            arrived(nearer)
            send(nearer, x_peer, 1, d + 1).start()
            send(nearer, core_peer, 2, d + 1).start()

        @pl.when(r == 1)
        def _():
            arrived(j)
            across = index_of(d, 1, 0)
            arrived(across)
            send(across, core_peer, 3, d).start()

        @pl.when(r == 3)
        def _():
            arrived(j)

        eig_copy(i).wait()
        inv[...] = 1.0 / (ev[j] + damping_shift)

        def form(q):
            products = jnp.dot(
                qleft[q], rights[j, pl.ds(0, qtok)], preferred_element_type=jnp.float32
            )
            precond[q % 2] = (products * inv[...]).astype(jnp.bfloat16)

        def contract(q):
            inner = jnp.dot(tleft[...], precond[q % 2], preferred_element_type=jnp.float32)
            inner = inner * rights[j, pl.ds(qtok, ttok)].astype(jnp.float32)
            folded = inner[:, :128]
            for lane in range(128, width, 128):
                folded = folded + inner[:, lane : lane + 128]
            acc[q] += folded

        form(0)
        for q in range(1, QUERIES):
            form(q)
            contract(q - 1)
        contract(QUERIES - 1)

    lanes = lax.broadcasted_iota(jnp.int32, (ttok, 128), 1)
    contrib = jnp.zeros((ttok, 128), jnp.float32)
    for q in range(QUERIES):
        contrib = jnp.where(lanes == q, jnp.sum(acc[q], axis=1, keepdims=True), contrib)
    labels = lax.broadcasted_iota(jnp.int32, (128, ttok), 0)
    onehot = jnp.where(labels == tids_ref[...], 1.0, 0.0)
    shares[me] = lax.dot_general(
        contrib.T[:QUERIES],
        onehot,
        (((1,), (1,)), ((), ())),
        precision=lax.Precision.HIGHEST,
        preferred_element_type=jnp.float32,
    )

    def share_copy(k, j):
        return pltpu.make_async_remote_copy(
            src_ref=shares.at[j],
            dst_ref=shares.at[j],
            send_sem=share_send.at[k],
            recv_sem=share_recv.at[j],
            device_id={"mp": (me + k) % MP},
        )

    @pl.loop(1, MP)
    def _(k):
        share_copy(k, me).start()

    for d in range(Z):
        if d > 0:
            send(me, index_of(d, 0, 0), 0, d).wait_send()
        send(me, x_peer, 1, d).wait_send()
        send(me, core_peer, 2, d).wait_send()
        send(me, core_peer, 3, d).wait_send()

    @pl.loop(1, MP)
    def _(k):
        share_copy(k, (me + k) % MP).wait_recv()

    @pl.loop(1, MP)
    def _(k):
        share_copy(k, me).wait_send()

    result = shares[0]
    for j in range(1, MP):
        result = result + shares[j]
    out_ref[...] = result[:, :TRAIN]


def fused_scores(qgrad, qin, qids, tgrad, tin, tids, obasis, ibasis, eig):
    qtok, depth = qin.shape
    ttok = tin.shape[0]
    width = ibasis.shape[1]
    tokens = qtok + ttok
    vmem = pl.BlockSpec(memory_space=pltpu.VMEM)
    hbm = pl.BlockSpec(memory_space=pl.ANY)
    dma = pltpu.SemaphoreType.DMA
    return pl.pallas_call(
        scores_kernel,
        out_shape=jax.ShapeDtypeStruct((QUERIES, TRAIN), jnp.float32),
        in_specs=[vmem, vmem] + [hbm] * 7,
        out_specs=vmem,
        scratch_shapes=[
            pltpu.VMEM((tokens, depth), jnp.bfloat16),
            pltpu.VMEM((tokens, depth), jnp.bfloat16),
            pltpu.VMEM((depth, width), jnp.bfloat16),
            pltpu.VMEM((depth, width), jnp.bfloat16),
            pltpu.VMEM((MP, width, width), jnp.float32),
            pltpu.VMEM((width, width), jnp.float32),
            pltpu.VMEM((2, width, width), jnp.bfloat16),
            pltpu.VMEM((tokens, width), jnp.float32),
            pltpu.VMEM((MP, tokens, width), jnp.bfloat16),
            pltpu.VMEM((QUERIES, width, qtok), jnp.bfloat16),
            pltpu.VMEM((ttok, width), jnp.bfloat16),
            pltpu.VMEM((QUERIES, ttok, 128), jnp.float32),
            pltpu.VMEM((MP, QUERIES, 128), jnp.float32),
            dma((4,)),
            dma((CHUNKS,)),
            dma((CHUNKS,)),
            dma((MP,)),
            dma((4, Z)),
            dma((MP,)),
            dma((MP,)),
            dma((MP,)),
        ],
        compiler_params=pltpu.CompilerParams(
            collective_id=0, has_side_effects=True, vmem_limit_bytes=56 * 2**20
        ),
    )(qids.reshape(1, qtok), tids.reshape(1, ttok), qgrad, qin, tgrad, tin, obasis, ibasis, eig)


def device_part(mp, qgrad, qin, qids, tgrad, tin, tids, obasis, ibasis, eig):
    run = fused_scores if mp == MP else on_device
    return run(qgrad, qin, qids, tgrad, tin, tids, obasis, ibasis, eig)


def solution(mesh):
    return jax.shard_map(
        functools.partial(device_part, mesh.shape["mp"]),
        mesh=mesh,
        in_specs=(
            P("grp", None),
            P("grp", None),
            P("grp"),
            P("grp", None),
            P("grp", None),
            P("grp"),
            P(None, "mp"),
            P(None, "mp"),
            P("mp", None),
        ),
        out_specs=P("grp", None),
        check_vma=False,
    )
```

```python
import functools
import math

import jax
import jax.numpy as jnp
from jax import lax
from jax.experimental import pallas as pl
from jax.experimental.pallas import tpu as pltpu
from jax.sharding import PartitionSpec as P

QUERIES = 8
QMOST = 8
TRAIN = 16


damping_shift = 0.25


def rotate(basis, factors):
    return lax.dot_general(
        basis, factors, (((0,), (1,)), ((), ())), preferred_element_type=jnp.float32
    ).astype(jnp.bfloat16)


def query_window(query_ids):
    token_count = query_ids.shape[0]
    labels = jnp.arange(QUERIES, dtype=jnp.int32)
    starts = jnp.sum((query_ids[None, :] < labels[:, None]).astype(jnp.int32), axis=1)
    window = jnp.minimum(
        starts[:, None] + jnp.arange(QMOST, dtype=jnp.int32)[None, :], token_count - 1
    )
    live_slot = jnp.take(query_ids, window) == labels[:, None]
    return (window, live_slot)


def window_rows(columns, window):
    return jnp.transpose(jnp.take(columns, window, axis=1), (1, 2, 0))


def build_precond(left_window, right_cols, eig_cols, window):
    right_window = window_rows(right_cols, window)
    query_count = left_window.shape[0]
    group_size = math.gcd(query_count, 8)
    left_groups = left_window.reshape(
        (query_count // group_size, group_size) + left_window.shape[1:]
    )
    right_groups = right_window.reshape(
        (query_count // group_size, group_size) + right_window.shape[1:]
    )

    def one_group(operands):
        products = jnp.einsum(
            "qms,qma->qsa", operands[0], operands[1], preferred_element_type=jnp.float32
        )
        return (products / (eig_cols[None] + damping_shift)).astype(jnp.bfloat16)

    precond_groups = lax.map(one_group, (left_groups, right_groups))
    return precond_groups.reshape((query_count,) + precond_groups.shape[2:])


def on_device(
    query_grad,
    query_input,
    query_ids,
    train_grad,
    train_input,
    train_ids,
    output_basis,
    input_basis,
    eigenvalues,
):
    query_left = rotate(output_basis, query_grad)
    query_right = rotate(input_basis, query_input)
    train_left = rotate(output_basis, train_grad)
    train_right = rotate(input_basis, train_input)
    window, live_slot = query_window(query_ids)
    left_taken = window_rows(query_left, window)
    left_window = jnp.where(live_slot[:, :, None], left_taken, jnp.zeros((), jnp.bfloat16))
    right_full, train_full = (
        lax.all_gather(query_right, "mp", axis=0, tiled=True),
        lax.all_gather(train_right, "mp", axis=0, tiled=True),
    )
    precond = build_precond(left_window, right_full, eigenvalues, window)
    inner_sum = jnp.einsum("qsa,at->qst", precond, train_full, preferred_element_type=jnp.float32)
    contrib = jnp.einsum(
        "qst,st->qt", inner_sum, train_left.astype(jnp.float32), precision=lax.Precision.HIGHEST
    )
    onehot = (train_ids[:, None] == jnp.arange(TRAIN, dtype=jnp.int32)[None, :]).astype(jnp.float32)
    shares = jnp.dot(contrib, onehot, precision=lax.Precision.HIGHEST)
    return lax.psum(shares, "mp")


Z, X, C = 4, 2, 2
MP = Z * X * C
CHUNKS = 8


def scores_kernel(
    qids_ref,
    tids_ref,
    qgrad,
    qin,
    tgrad,
    tin,
    obasis,
    ibasis,
    eig,
    out_ref,
    in_rows,
    grad_rows,
    ib,
    ob,
    ev,
    inv,
    precond,
    total,
    rights,
    qleft,
    tleft,
    acc,
    shares,
    row_sem,
    ib_sem,
    ob_sem,
    ev_sem,
    send_sem,
    recv_sem,
    share_send,
    share_recv,
):
    me = lax.axis_index("mp")
    z, x, c = me // (X * C), (me // C) % X, me % C
    qtok, depth = qin.shape
    ttok = tin.shape[0]
    width = ibasis.shape[1]
    chunk = depth // CHUNKS

    upper, inner_z = z // 2, (z + 1) // 2 % 2

    def z_source(k):
        place = k + inner_z * (1 - 2 * (k % 2)) * (1 - k // 2)
        return place * (1 - 2 * upper) + (Z - 1) * upper

    def index_at(at_z, dx, dc):
        return (at_z * X + (x + dx) % X) * C + (c + dc) % C

    def index_of(k, dx, dc):
        return index_at(z_source(k), dx, dc)

    def row_copies(q, t, rows, k):
        return (
            pltpu.make_async_copy(q, rows.at[pl.ds(0, qtok)], row_sem.at[k]),
            pltpu.make_async_copy(t, rows.at[pl.ds(qtok, ttok)], row_sem.at[k + 1]),
        )

    def basis_copy(source, target, sem, k):
        part = pl.ds(pl.multiple_of(k * chunk, chunk), chunk)
        return pltpu.make_async_copy(source.at[part], target.at[part], sem.at[k])

    def block_index(i):
        return index_of(i // 4, i % 4 // 2, i % 2)

    def eig_copy(i):
        j = block_index(i)
        part = pl.ds(pl.multiple_of(j * width, width), width)
        return pltpu.make_async_copy(eig.at[:, part], ev.at[j], ev_sem.at[j])

    for copy in row_copies(qin, tin, in_rows, 0):
        copy.start()
    for k in range(CHUNKS):
        basis_copy(ibasis, ib, ib_sem, k).start()
    for copy in row_copies(qgrad, tgrad, grad_rows, 2):
        copy.start()

    barrier = pltpu.get_barrier_semaphore()

    @pl.loop(1, MP)
    def _(k):
        pl.semaphore_signal(barrier, inc=1, device_id={"mp": (me + k) % MP})

    def rotate_rows(rows, basis, wait_chunk):
        total[...] = jnp.zeros_like(total)

        @pl.loop(0, CHUNKS)
        def _(k):
            wait_chunk(k)
            part = pl.ds(pl.multiple_of(k * chunk, chunk), chunk)
            total[...] += jnp.dot(rows[:, part], basis[part, :], preferred_element_type=jnp.float32)

    def wait_in(k):
        basis_copy(ibasis, ib, ib_sem, k).wait()
        basis_copy(obasis, ob, ob_sem, k).start()

    def wait_out(k):
        basis_copy(obasis, ob, ob_sem, k).wait()
        eig_copy(2 * k).start()
        eig_copy(2 * k + 1).start()

    for copy in row_copies(qin, tin, in_rows, 0):
        copy.wait()
    rotate_rows(in_rows, ib, wait_in)
    rights[me] = total[...].astype(jnp.bfloat16)

    pl.semaphore_wait(barrier, MP - 1)

    def send(j, peer, kind, d):
        return pltpu.make_async_remote_copy(
            src_ref=rights.at[j],
            dst_ref=rights.at[j],
            send_sem=send_sem.at[kind, d],
            recv_sem=recv_sem.at[j],
            device_id={"mp": peer},
        )

    x_peer, core_peer = index_of(0, 1, 0), index_of(0, 0, 1)
    send(me, core_peer, 2, 0).start()
    send(me, x_peer, 1, 0).start()

    @pl.when(z < Z - 1)
    def _():
        send(me, index_at(z + 1, 0, 0), 0, 0).start()

    @pl.when(z > 0)
    def _():
        send(me, index_at(z - 1, 0, 0), 4, 0).start()

    for copy in row_copies(qgrad, tgrad, grad_rows, 2):
        copy.wait()
    rotate_rows(grad_rows, ob, wait_out)
    tleft[...] = total[pl.ds(qtok, ttok), :].astype(jnp.bfloat16)
    turned = total[pl.ds(0, 128), :].astype(jnp.bfloat16).astype(jnp.float32).T[:, :qtok]
    qids = qids_ref[...]
    last = lax.broadcasted_iota(jnp.int32, (1, qtok), 1) == qtok - 1
    for q in range(QUERIES):
        start = jnp.sum(jnp.where(qids < q, 1.0, 0.0), axis=1, keepdims=True)
        repeats = jnp.where(last, start + (QMOST - qtok + 1), 1.0)
        weights = jnp.where(qids == q, repeats, 0.0)
        qleft[q] = (turned * weights).astype(jnp.bfloat16)
    acc[...] = jnp.zeros_like(acc)

    def arrived(j):
        send(j, core_peer, 0, 0).wait_recv()

    @pl.loop(0, MP)
    def _(i):
        d, r = i // 4, i % 4
        j = block_index(i)

        def pass_on(k):
            source_z = z_source(k)
            block = index_at(source_z, 0, 0)
            arrived(block)

            @pl.when(jnp.logical_and(inner_z == 1, source_z < z))
            def _():
                send(block, index_at(z + 1, 0, 0), 0, k).start()

            @pl.when(jnp.logical_and(inner_z == 1, source_z > z))
            def _():
                send(block, index_at(z - 1, 0, 0), 0, k).start()

            send(block, x_peer, 1, k).start()
            send(block, core_peer, 2, k).start()

        for k in range(1, Z):

            @pl.when(i == 2 * (k - 1) - inner_z * ((k - 1) * 2 - k // 3 * 2))
            def _():
                pass_on(k)

        @pl.when(r == 1)
        def _():
            arrived(j)
            across = index_of(d, 1, 0)
            arrived(across)
            send(across, core_peer, 3, d).start()

        @pl.when(r == 3)
        def _():
            arrived(j)

        eig_copy(i).wait()
        inv[...] = 1.0 / (ev[j] + damping_shift)

        def form(q):
            products = jnp.dot(
                qleft[q], rights[j, pl.ds(0, qtok)], preferred_element_type=jnp.float32
            )
            precond[q % 2] = (products * inv[...]).astype(jnp.bfloat16)

        def contract(q):
            inner = jnp.dot(tleft[...], precond[q % 2], preferred_element_type=jnp.float32)
            inner = inner * rights[j, pl.ds(qtok, ttok)].astype(jnp.float32)
            folded = inner[:, :128]
            for lane in range(128, width, 128):
                folded = folded + inner[:, lane : lane + 128]
            acc[q] += folded

        form(0)
        for q in range(1, QUERIES):
            form(q)
            contract(q - 1)
        contract(QUERIES - 1)

    lanes = lax.broadcasted_iota(jnp.int32, (ttok, 128), 1)
    contrib = jnp.zeros((ttok, 128), jnp.float32)
    for q in range(QUERIES):
        contrib = jnp.where(lanes == q, jnp.sum(acc[q], axis=1, keepdims=True), contrib)
    labels = lax.broadcasted_iota(jnp.int32, (128, ttok), 0)
    onehot = jnp.where(labels == tids_ref[...], 1.0, 0.0)
    shares[me] = lax.dot_general(
        contrib.T[:QUERIES],
        onehot,
        (((1,), (1,)), ((), ())),
        precision=lax.Precision.HIGHEST,
        preferred_element_type=jnp.float32,
    )

    def share_copy(k, j):
        return pltpu.make_async_remote_copy(
            src_ref=shares.at[j],
            dst_ref=shares.at[j],
            send_sem=share_send.at[k],
            recv_sem=share_recv.at[j],
            device_id={"mp": (me + k) % MP},
        )

    @pl.loop(1, MP)
    def _(k):
        share_copy(k, me).start()

    @pl.when(z < Z - 1)
    def _():
        send(me, core_peer, 0, 0).wait_send()

    @pl.when(z > 0)
    def _():
        send(me, core_peer, 4, 0).wait_send()

    for d in range(Z):
        if d > 0:

            @pl.when(inner_z == 1)
            def _():
                send(me, core_peer, 0, d).wait_send()

        send(me, x_peer, 1, d).wait_send()
        send(me, core_peer, 2, d).wait_send()
        send(me, core_peer, 3, d).wait_send()

    @pl.loop(1, MP)
    def _(k):
        share_copy(k, (me + k) % MP).wait_recv()

    @pl.loop(1, MP)
    def _(k):
        share_copy(k, me).wait_send()

    result = shares[0]
    for j in range(1, MP):
        result = result + shares[j]
    out_ref[...] = result[:, :TRAIN]


def fused_scores(qgrad, qin, qids, tgrad, tin, tids, obasis, ibasis, eig):
    qtok, depth = qin.shape
    ttok = tin.shape[0]
    width = ibasis.shape[1]
    tokens = qtok + ttok
    vmem = pl.BlockSpec(memory_space=pltpu.VMEM)
    hbm = pl.BlockSpec(memory_space=pl.ANY)
    dma = pltpu.SemaphoreType.DMA
    return pl.pallas_call(
        scores_kernel,
        out_shape=jax.ShapeDtypeStruct((QUERIES, TRAIN), jnp.float32),
        in_specs=[vmem, vmem] + [hbm] * 7,
        out_specs=vmem,
        scratch_shapes=[
            pltpu.VMEM((tokens, depth), jnp.bfloat16),
            pltpu.VMEM((tokens, depth), jnp.bfloat16),
            pltpu.VMEM((depth, width), jnp.bfloat16),
            pltpu.VMEM((depth, width), jnp.bfloat16),
            pltpu.VMEM((MP, width, width), jnp.float32),
            pltpu.VMEM((width, width), jnp.float32),
            pltpu.VMEM((2, width, width), jnp.bfloat16),
            pltpu.VMEM((tokens, width), jnp.float32),
            pltpu.VMEM((MP, tokens, width), jnp.bfloat16),
            pltpu.VMEM((QUERIES, width, qtok), jnp.bfloat16),
            pltpu.VMEM((ttok, width), jnp.bfloat16),
            pltpu.VMEM((QUERIES, ttok, 128), jnp.float32),
            pltpu.VMEM((MP, QUERIES, 128), jnp.float32),
            dma((4,)),
            dma((CHUNKS,)),
            dma((CHUNKS,)),
            dma((MP,)),
            dma((5, Z)),
            dma((MP,)),
            dma((MP,)),
            dma((MP,)),
        ],
        compiler_params=pltpu.CompilerParams(
            collective_id=0, has_side_effects=True, vmem_limit_bytes=56 * 2**20
        ),
    )(qids.reshape(1, qtok), tids.reshape(1, ttok), qgrad, qin, tgrad, tin, obasis, ibasis, eig)


def device_part(mp, qgrad, qin, qids, tgrad, tin, tids, obasis, ibasis, eig):
    run = fused_scores if mp == MP else on_device
    return run(qgrad, qin, qids, tgrad, tin, tids, obasis, ibasis, eig)


def solution(mesh):
    return jax.shard_map(
        functools.partial(device_part, mesh.shape["mp"]),
        mesh=mesh,
        in_specs=(
            P("grp", None),
            P("grp", None),
            P("grp"),
            P("grp", None),
            P("grp", None),
            P("grp"),
            P(None, "mp"),
            P(None, "mp"),
            P("mp", None),
        ),
        out_specs=P("grp", None),
        check_vma=False,
    )
```

```python
import functools
import math

import jax
import jax.numpy as jnp
from jax import lax
from jax.experimental import pallas as pl
from jax.experimental.pallas import tpu as pltpu
from jax.sharding import PartitionSpec as P

QUERIES = 8
QMOST = 8
TRAIN = 16


damping_shift = 0.25


def rotate(basis, factors):
    return lax.dot_general(
        basis, factors, (((0,), (1,)), ((), ())), preferred_element_type=jnp.float32
    ).astype(jnp.bfloat16)


def query_window(query_ids):
    token_count = query_ids.shape[0]
    labels = jnp.arange(QUERIES, dtype=jnp.int32)
    starts = jnp.sum((query_ids[None, :] < labels[:, None]).astype(jnp.int32), axis=1)
    window = jnp.minimum(
        starts[:, None] + jnp.arange(QMOST, dtype=jnp.int32)[None, :], token_count - 1
    )
    live_slot = jnp.take(query_ids, window) == labels[:, None]
    return (window, live_slot)


def window_rows(columns, window):
    return jnp.transpose(jnp.take(columns, window, axis=1), (1, 2, 0))


def build_precond(left_window, right_cols, eig_cols, window):
    right_window = window_rows(right_cols, window)
    query_count = left_window.shape[0]
    group_size = math.gcd(query_count, 8)
    left_groups = left_window.reshape(
        (query_count // group_size, group_size) + left_window.shape[1:]
    )
    right_groups = right_window.reshape(
        (query_count // group_size, group_size) + right_window.shape[1:]
    )

    def one_group(operands):
        products = jnp.einsum(
            "qms,qma->qsa", operands[0], operands[1], preferred_element_type=jnp.float32
        )
        return (products / (eig_cols[None] + damping_shift)).astype(jnp.bfloat16)

    precond_groups = lax.map(one_group, (left_groups, right_groups))
    return precond_groups.reshape((query_count,) + precond_groups.shape[2:])


def on_device(
    query_grad,
    query_input,
    query_ids,
    train_grad,
    train_input,
    train_ids,
    output_basis,
    input_basis,
    eigenvalues,
):
    query_left = rotate(output_basis, query_grad)
    query_right = rotate(input_basis, query_input)
    train_left = rotate(output_basis, train_grad)
    train_right = rotate(input_basis, train_input)
    window, live_slot = query_window(query_ids)
    left_taken = window_rows(query_left, window)
    left_window = jnp.where(live_slot[:, :, None], left_taken, jnp.zeros((), jnp.bfloat16))
    right_full, train_full = (
        lax.all_gather(query_right, "mp", axis=0, tiled=True),
        lax.all_gather(train_right, "mp", axis=0, tiled=True),
    )
    precond = build_precond(left_window, right_full, eigenvalues, window)
    inner_sum = jnp.einsum("qsa,at->qst", precond, train_full, preferred_element_type=jnp.float32)
    contrib = jnp.einsum(
        "qst,st->qt", inner_sum, train_left.astype(jnp.float32), precision=lax.Precision.HIGHEST
    )
    onehot = (train_ids[:, None] == jnp.arange(TRAIN, dtype=jnp.int32)[None, :]).astype(jnp.float32)
    shares = jnp.dot(contrib, onehot, precision=lax.Precision.HIGHEST)
    return lax.psum(shares, "mp")


Z, X, C = 4, 2, 2
MP = Z * X * C
CHUNKS = 8


def scores_kernel(
    qids_ref,
    tids_ref,
    qgrad,
    qin,
    tgrad,
    tin,
    obasis,
    ibasis,
    eig,
    out_ref,
    in_rows,
    grad_rows,
    ib,
    ob,
    ev,
    inv,
    precond,
    total,
    rights,
    qleft,
    tleft,
    acc,
    shares,
    row_sem,
    ib_sem,
    ob_sem,
    ev_sem,
    send_sem,
    recv_sem,
    share_send,
    share_recv,
):
    me = lax.axis_index("mp")
    z, x, c = me // (X * C), (me // C) % X, me % C
    qtok, depth = qin.shape
    ttok = tin.shape[0]
    width = ibasis.shape[1]
    chunk = depth // CHUNKS

    upper, inner_z = z // 2, (z + 1) // 2 % 2

    def z_source(k):
        place = k + inner_z * (1 - 2 * (k % 2)) * (1 - k // 2)
        return place * (1 - 2 * upper) + (Z - 1) * upper

    def index_at(at_z, dx, dc):
        return (at_z * X + (x + dx) % X) * C + (c + dc) % C

    def index_of(k, dx, dc):
        return index_at(z_source(k), dx, dc)

    def row_copies(q, t, rows, k):
        return (
            pltpu.make_async_copy(q, rows.at[pl.ds(0, qtok)], row_sem.at[k]),
            pltpu.make_async_copy(t, rows.at[pl.ds(qtok, ttok)], row_sem.at[k + 1]),
        )

    def basis_copy(source, target, sem, k):
        part = pl.ds(pl.multiple_of(k * chunk, chunk), chunk)
        return pltpu.make_async_copy(source.at[part], target.at[part], sem.at[k])

    def block_index(i):
        return index_of(i // 4, i % 4 // 2, i % 2)

    def eig_copy(i):
        j = block_index(i)
        part = pl.ds(pl.multiple_of(j * width, width), width)
        return pltpu.make_async_copy(eig.at[:, part], ev.at[j], ev_sem.at[j])

    for copy in row_copies(qin, tin, in_rows, 0):
        copy.start()
    for k in range(CHUNKS):
        basis_copy(ibasis, ib, ib_sem, k).start()
    for copy in row_copies(qgrad, tgrad, grad_rows, 2):
        copy.start()

    barrier = pltpu.get_barrier_semaphore()

    @pl.loop(1, MP)
    def _(k):
        pl.semaphore_signal(barrier, inc=1, device_id={"mp": (me + k) % MP})

    def rotate_rows(rows, basis, wait_chunk):
        total[...] = jnp.zeros_like(total)

        @pl.loop(0, CHUNKS)
        def _(k):
            wait_chunk(k)
            part = pl.ds(pl.multiple_of(k * chunk, chunk), chunk)
            total[...] += jnp.dot(rows[:, part], basis[part, :], preferred_element_type=jnp.float32)

    def wait_in(k):
        basis_copy(ibasis, ib, ib_sem, k).wait()
        basis_copy(obasis, ob, ob_sem, k).start()

    def wait_out(k):
        basis_copy(obasis, ob, ob_sem, k).wait()
        eig_copy(2 * k).start()
        eig_copy(2 * k + 1).start()

    for copy in row_copies(qin, tin, in_rows, 0):
        copy.wait()
    rotate_rows(in_rows, ib, wait_in)
    rights[me] = total[...].astype(jnp.bfloat16)

    pl.semaphore_wait(barrier, MP - 1)

    def send(j, peer, kind, d):
        return pltpu.make_async_remote_copy(
            src_ref=rights.at[j],
            dst_ref=rights.at[j],
            send_sem=send_sem.at[kind, d],
            recv_sem=recv_sem.at[j],
            device_id={"mp": peer},
        )

    x_peer, core_peer = index_of(0, 1, 0), index_of(0, 0, 1)
    send(me, core_peer, 2, 0).start()
    send(me, x_peer, 1, 0).start()

    @pl.when(z < Z - 1)
    def _():
        send(me, index_at(z + 1, 0, 0), 0, 0).start()

    @pl.when(z > 0)
    def _():
        send(me, index_at(z - 1, 0, 0), 4, 0).start()

    for copy in row_copies(qgrad, tgrad, grad_rows, 2):
        copy.wait()
    rotate_rows(grad_rows, ob, wait_out)
    tleft[...] = total[pl.ds(qtok, ttok), :].astype(jnp.bfloat16)
    turned = total[pl.ds(0, 128), :].astype(jnp.bfloat16).astype(jnp.float32).T[:, :qtok]
    qids = qids_ref[...]
    last = lax.broadcasted_iota(jnp.int32, (1, qtok), 1) == qtok - 1
    for q in range(QUERIES):
        start = jnp.sum(jnp.where(qids < q, 1.0, 0.0), axis=1, keepdims=True)
        repeats = jnp.where(last, start + (QMOST - qtok + 1), 1.0)
        weights = jnp.where(qids == q, repeats, 0.0)
        qleft[q] = (turned * weights).astype(jnp.bfloat16)
    acc[...] = jnp.zeros_like(acc)

    def arrived(j):
        send(j, core_peer, 0, 0).wait_recv()

    @pl.loop(0, MP)
    def _(i):
        d, r = i // 4, i % 4
        j = block_index(i)

        def pass_on(k):
            source_z = z_source(k)
            block = index_at(source_z, 0, 0)
            arrived(block)

            @pl.when(jnp.logical_and(inner_z == 1, source_z < z))
            def _():
                send(block, index_at(z + 1, 0, 0), 0, k).start()

            @pl.when(jnp.logical_and(inner_z == 1, source_z > z))
            def _():
                send(block, index_at(z - 1, 0, 0), 0, k).start()

            send(block, x_peer, 1, k).start()
            send(block, core_peer, 2, k).start()

        for k in range(1, Z):

            @pl.when(i == 4 * k - 3 - inner_z * (0, 0, 3, 4)[k])
            def _():
                pass_on(k)

        @pl.when(r == 1)
        def _():
            arrived(j)
            across = index_of(d, 1, 0)
            arrived(across)
            send(across, core_peer, 3, d).start()

        @pl.when(r == 3)
        def _():
            arrived(j)

        eig_copy(i).wait()
        inv[...] = 1.0 / (ev[j] + damping_shift)

        def form(q):
            products = jnp.dot(
                qleft[q], rights[j, pl.ds(0, qtok)], preferred_element_type=jnp.float32
            )
            precond[q % 2] = (products * inv[...]).astype(jnp.bfloat16)

        def contract(q):
            inner = jnp.dot(tleft[...], precond[q % 2], preferred_element_type=jnp.float32)
            inner = inner * rights[j, pl.ds(qtok, ttok)].astype(jnp.float32)
            folded = inner[:, :128]
            for lane in range(128, width, 128):
                folded = folded + inner[:, lane : lane + 128]
            acc[q] += folded

        form(0)
        for q in range(1, QUERIES):
            form(q)
            contract(q - 1)
        contract(QUERIES - 1)

    lanes = lax.broadcasted_iota(jnp.int32, (ttok, 128), 1)
    contrib = jnp.zeros((ttok, 128), jnp.float32)
    for q in range(QUERIES):
        contrib = jnp.where(lanes == q, jnp.sum(acc[q], axis=1, keepdims=True), contrib)
    labels = lax.broadcasted_iota(jnp.int32, (128, ttok), 0)
    onehot = jnp.where(labels == tids_ref[...], 1.0, 0.0)
    shares[me] = lax.dot_general(
        contrib.T[:QUERIES],
        onehot,
        (((1,), (1,)), ((), ())),
        precision=lax.Precision.HIGHEST,
        preferred_element_type=jnp.float32,
    )

    def share_copy(k, j):
        return pltpu.make_async_remote_copy(
            src_ref=shares.at[j],
            dst_ref=shares.at[j],
            send_sem=share_send.at[k],
            recv_sem=share_recv.at[j],
            device_id={"mp": (me + k) % MP},
        )

    @pl.loop(1, MP)
    def _(k):
        share_copy(k, me).start()

    @pl.when(z < Z - 1)
    def _():
        send(me, core_peer, 0, 0).wait_send()

    @pl.when(z > 0)
    def _():
        send(me, core_peer, 4, 0).wait_send()

    for d in range(Z):
        if d > 0:

            @pl.when(inner_z == 1)
            def _():
                send(me, core_peer, 0, d).wait_send()

        send(me, x_peer, 1, d).wait_send()
        send(me, core_peer, 2, d).wait_send()
        send(me, core_peer, 3, d).wait_send()

    @pl.loop(1, MP)
    def _(k):
        share_copy(k, (me + k) % MP).wait_recv()

    @pl.loop(1, MP)
    def _(k):
        share_copy(k, me).wait_send()

    result = shares[0]
    for j in range(1, MP):
        result = result + shares[j]
    out_ref[...] = result[:, :TRAIN]


def fused_scores(qgrad, qin, qids, tgrad, tin, tids, obasis, ibasis, eig):
    qtok, depth = qin.shape
    ttok = tin.shape[0]
    width = ibasis.shape[1]
    tokens = qtok + ttok
    vmem = pl.BlockSpec(memory_space=pltpu.VMEM)
    hbm = pl.BlockSpec(memory_space=pl.ANY)
    dma = pltpu.SemaphoreType.DMA
    return pl.pallas_call(
        scores_kernel,
        out_shape=jax.ShapeDtypeStruct((QUERIES, TRAIN), jnp.float32),
        in_specs=[vmem, vmem] + [hbm] * 7,
        out_specs=vmem,
        scratch_shapes=[
            pltpu.VMEM((tokens, depth), jnp.bfloat16),
            pltpu.VMEM((tokens, depth), jnp.bfloat16),
            pltpu.VMEM((depth, width), jnp.bfloat16),
            pltpu.VMEM((depth, width), jnp.bfloat16),
            pltpu.VMEM((MP, width, width), jnp.float32),
            pltpu.VMEM((width, width), jnp.float32),
            pltpu.VMEM((2, width, width), jnp.bfloat16),
            pltpu.VMEM((tokens, width), jnp.float32),
            pltpu.VMEM((MP, tokens, width), jnp.bfloat16),
            pltpu.VMEM((QUERIES, width, qtok), jnp.bfloat16),
            pltpu.VMEM((ttok, width), jnp.bfloat16),
            pltpu.VMEM((QUERIES, ttok, 128), jnp.float32),
            pltpu.VMEM((MP, QUERIES, 128), jnp.float32),
            dma((4,)),
            dma((CHUNKS,)),
            dma((CHUNKS,)),
            dma((MP,)),
            dma((5, Z)),
            dma((MP,)),
            dma((MP,)),
            dma((MP,)),
        ],
        compiler_params=pltpu.CompilerParams(
            collective_id=0, has_side_effects=True, vmem_limit_bytes=56 * 2**20
        ),
    )(qids.reshape(1, qtok), tids.reshape(1, ttok), qgrad, qin, tgrad, tin, obasis, ibasis, eig)


def device_part(mp, qgrad, qin, qids, tgrad, tin, tids, obasis, ibasis, eig):
    run = fused_scores if mp == MP else on_device
    return run(qgrad, qin, qids, tgrad, tin, tids, obasis, ibasis, eig)


def solution(mesh):
    return jax.shard_map(
        functools.partial(device_part, mesh.shape["mp"]),
        mesh=mesh,
        in_specs=(
            P("grp", None),
            P("grp", None),
            P("grp"),
            P("grp", None),
            P("grp", None),
            P("grp"),
            P(None, "mp"),
            P(None, "mp"),
            P("mp", None),
        ),
        out_specs=P("grp", None),
        check_vma=False,
    )
```
